32 devices in a mesh: hi: 4 (over x, core), lo: 8 (over z, y).
Axes of the slice: x: 2, y: 2, z: 4, core: 2. Of those that a mesh axis runs over, the one named last changes fastest.
Arguments:
- blocks: bfloat16 [2048, 128, 128], P(('hi', 'lo')), may hold values from -6 to 6
- diag_factors: bfloat16 [4, 2048, 128, 128], P(None, ('hi', 'lo')), may hold values from -0.375 to 0.375
- off_factors: bfloat16 [4, 2048, 128, 128], P(None, ('hi', 'lo')), may hold values from -0.375 to 0.375
- partner_maps: int32 [4, 64], replicated, may hold values from 0 to 63, each once within a row
Outputs:
- summed: bfloat16 [512, 128, 128], P(('lo', 'hi'))
The draws below stay inside these ranges and needn't reach their ends.
Inputs may be any that keep to these rules, and one draw needn't show every extreme that they name: Each row of partner_maps is a permutation of 0 to 63.
All inputs are finite; a program needn't handle non-finite values.
Results may differ from the reference program's by a relative error of at most 0.009.
Values may be sent and summed in bfloat16 or wider, within the bound.
A program may use at most 128 MiB of HBM per device.

```python
import jax
import jax.numpy as jnp
import numpy as np

P_SIZE = 128
R = 128
LEVELS = 4
BLK_DEV = 64
NBLK = 2048
N_HI = 4
N_LO = 8


def levels(own_key, extent, cuts, smallest, largest):
    def one(position, shards_of):
        steps = jax.random.uniform(jax.random.fold_in(jax.random.fold_in(own_key, 6), position), (shards_of,), jnp.float32, smallest / len(cuts), largest / len(cuts))
        return jnp.repeat(jnp.exp(steps), extent[position] // shards_of).reshape((-1,) + (1,) * (len(extent) - position - 1))

    loudness = one(*cuts[0])
    for cut in cuts[1:]:
        loudness = loudness * one(*cut)
    return loudness


def noise(stream_key, extent, spread, reach, split=(), held_as=jnp.bfloat16):
    gain = levels(stream_key, extent, split, -0.22, 0.18) if split else 1.0
    array = jax.random.normal(stream_key, extent, jnp.float32) * spread * gain
    return jnp.minimum(jnp.maximum(array, -reach), reach).astype(held_as)


def setup_inputs(seed: int = 0) -> dict:
    seeds = jax.random.split(jax.random.key(seed), 5)
    blocks = noise(seeds[0], (NBLK, R, P_SIZE), 1.0, 6.0, ((0, 32),))
    diag_factors = noise(seeds[1], (LEVELS, NBLK, P_SIZE, P_SIZE), (2 * P_SIZE) ** -0.5, 0.375, ((1, 32),))
    off_factors = noise(seeds[2], (LEVELS, NBLK, P_SIZE, P_SIZE), (2 * P_SIZE) ** -0.5, 0.375, ((1, 32),))
    partner_maps = jax.vmap(lambda own: jax.random.permutation(own, BLK_DEV))(jax.random.split(seeds[3], LEVELS)).reshape((LEVELS, BLK_DEV)).astype(jnp.int32)
    return {"blocks": blocks, "diag_factors": diag_factors, "off_factors": off_factors, "partner_maps": partner_maps}


def apply_factor(factor, data):
    return jnp.einsum("hlbij,hlbrj->hlbri", factor.astype(jnp.float32), data.astype(jnp.float32))


def reference(blocks, diag_factors, off_factors, partner_maps):
    current = blocks.reshape(N_HI, N_LO, BLK_DEV, R, P_SIZE)
    top = N_LO.bit_length() - 1
    for level, bit in enumerate((0, 1, top - 1)):
        order = np.arange(N_LO) ^ (1 << bit)
        partner = current[:, order]
        partner = jnp.take(partner, partner_maps[level].astype(jnp.int32), axis=2)
        diag = diag_factors[level].reshape(N_HI, N_LO, BLK_DEV, P_SIZE, P_SIZE)
        off = off_factors[level].reshape(N_HI, N_LO, BLK_DEV, P_SIZE, P_SIZE)
        mixed = apply_factor(diag, current) + apply_factor(off, partner)
        current = mixed.astype(jnp.bfloat16)
    own = apply_factor(diag_factors[3].reshape(N_HI, N_LO, BLK_DEV, P_SIZE, P_SIZE), current)
    moved = apply_factor(off_factors[3].reshape(N_HI, N_LO, BLK_DEV, P_SIZE, P_SIZE), current)
    order = np.arange(N_HI) ^ 2
    moved = jnp.take(moved[order], partner_maps[3].astype(jnp.int32), axis=2)
    total = jnp.sum(own + moved, axis=0)
    return total.reshape(N_LO * BLK_DEV, R, P_SIZE).astype(jnp.bfloat16)
```

```python
import functools

import jax
import jax.numpy as jnp
from jax import lax
from jax.experimental import pallas as pl
from jax.experimental.pallas import tpu as pltpu
from jax.sharding import PartitionSpec as P

MESH = pl.DeviceIdType.MESH
UNROLL = 8


def chunk_plan(rows):
    unit = rows // 8
    sizes = (unit, 2 * unit, 2 * unit, 2 * unit, unit)
    starts = [sum(sizes[:i]) for i in range(len(sizes))]
    return tuple(zip(starts, sizes))


def order_of(chunks):
    y_free = z_free = mid_free = 0.0
    times = []
    for c, (_, size) in enumerate(chunks):
        y_free = y_free + size
        times.append((y_free, 0, c))
        z_free = max(z_free, y_free) + size * (1.0 if c == 0 else 1.5)
        times.append((z_free, 1, c))
        mid_free = max(mid_free, z_free) + 2 * size
        times.append((mid_free, 2, c))
    return [(level, c) for _, level, c in sorted(times)]


def flip(index, step):
    return index + step * (1 - 2 * (lax.rem(lax.div(index, step), 2)))


def kernel(n_hi, n_lo, chunks, maps, blocks, diag, off, out, *scratch):
    count = len(chunks)
    scratch = list(scratch)

    def take(number):
        taken = scratch[:number]
        del scratch[:number]
        return taken

    x0, = take(1)
    xs = [None] + [take(count) for _ in range(3)]
    recv = [take(count) for _ in range(3)]
    partial = take(count)
    others = take(count)
    dfs = take(4)
    ofs = take(4)
    load_sem, factor_sem, send_sem, recv_sem, sum_send, sum_recv = scratch

    hi = lax.axis_index("hi")
    lo = lax.axis_index("lo")
    steps = (1, 2, n_lo // 2)
    nblk = blocks.shape[0]
    share = nblk // n_hi

    near = sorted(set(steps))
    lo_partner = {s: flip(lo, s) for s in near}
    hi_partner = [lax.rem(hi + d, n_hi) for d in range(1, n_hi)]
    barrier = pltpu.get_barrier_semaphore()
    for s in near:
        pl.semaphore_signal(barrier, inc=1, device_id=(hi, lo_partner[s]), device_id_type=MESH)
    for h in hi_partner:
        pl.semaphore_signal(barrier, inc=1, device_id=(h, lo), device_id_type=MESH)

    load_x = pltpu.make_async_copy(blocks, x0, load_sem)
    load_x.start()
    loads = []
    for k in range(4):
        loads.append((
            pltpu.make_async_copy(diag.at[k], dfs[k], factor_sem.at[0, k]),
            pltpu.make_async_copy(off.at[k], ofs[k], factor_sem.at[1, k]),
        ))
    for copy in loads[0]:
        copy.start()
    pl.semaphore_wait(barrier, len(near) + n_hi - 1)

    def exchange(level, c):
        start, size = chunks[c]
        source = blocks.at[:, pl.ds(start, size), :] if level == 0 else xs[level][c]
        return pltpu.make_async_remote_copy(
            src_ref=source,
            dst_ref=recv[level][c],
            send_sem=send_sem.at[level, c],
            recv_sem=recv_sem.at[level, c],
            device_id=(hi, lo_partner[steps[level]]),
            device_id_type=MESH,
        )

    def hand_on(c, d):
        return pltpu.make_async_remote_copy(
            src_ref=partial[c].at[pl.ds(hi_partner[d] * share, share)],
            dst_ref=others[c].at[d],
            send_sem=sum_send.at[d, c],
            recv_sem=sum_recv.at[d, c],
            device_id=(hi_partner[d], lo),
            device_id_type=MESH,
        )

    def product(left, right, d, o):
        return lax.dot_general(
            jnp.concatenate([left, right], axis=1),
            jnp.concatenate([d, o], axis=1),
            (((1,), (1,)), ((), ())),
            preferred_element_type=jnp.float32,
        ).astype(jnp.bfloat16)

    def over_blocks(number, one):
        unroll = UNROLL if number % UNROLL == 0 else 1

        def some(i, _):
            for u in range(unroll):
                one(i * unroll + u)
            return 0

        lax.fori_loop(0, number // unroll, some, 0)

    def mix(level, c):
        start, size = chunks[c]

        def one(j):
            mine = x0[j, pl.ds(start, size), :] if level == 0 else xs[level][c][j]
            theirs = recv[level][c][maps[level, j]]
            xs[level + 1][c][j] = product(mine, theirs, dfs[level][j], ofs[level][j])

        over_blocks(nblk, one)

    def last(c):
        def one(j):
            p = maps[3, j]
            partial[c][j] = product(xs[3][c][j], xs[3][c][p], dfs[3][j], ofs[3][p])

        over_blocks(nblk, one)

    def gather_sum(c):
        start, size = chunks[c]
        for d in range(n_hi - 1):
            hand_on(c, d).wait_recv()

        def one(i):
            total = partial[c][hi * share + i].astype(jnp.float32)
            for d in range(n_hi - 1):
                total = total + others[c][d, i].astype(jnp.float32)
            out[i, pl.ds(start, size), :] = total.astype(jnp.bfloat16)

        over_blocks(share, one)

    exchange(0, 0).start()
    for k in range(1, 4):
        for copy in loads[k]:
            copy.start()
    load_x.wait()
    loaded = set()
    pending = []
    for level, c in order_of(chunks):
        exchange(level, c).wait_recv()
        if level == 0 and c + 1 < count:
            exchange(0, c + 1).start()
        if level not in loaded:
            for copy in loads[level]:
                copy.wait()
            loaded.add(level)
        mix(level, c)
        if level < 2:
            exchange(level + 1, c).start()
            continue
        if 3 not in loaded:
            for copy in loads[3]:
                copy.wait()
            loaded.add(3)
        last(c)
        for d in range(n_hi - 1):
            hand_on(c, d).start()
        for earlier in pending:
            gather_sum(earlier)
        pending = [c]
    for earlier in pending:
        gather_sum(earlier)
    for c in range(count):
        for level in range(3):
            exchange(level, c).wait_send()
        for d in range(n_hi - 1):
            hand_on(c, d).wait_send()


def body(n_hi, n_lo, blocks, diag_factors, off_factors, partner_maps):
    nblk, rows, width = blocks.shape
    chunks = chunk_plan(rows)
    count = len(chunks)
    share = nblk // n_hi
    bf16 = jnp.bfloat16
    whole = pltpu.VMEM((nblk, rows, width), bf16)
    pieces = [pltpu.VMEM((nblk, size, width), bf16) for _, size in chunks]
    shares = [pltpu.VMEM((n_hi - 1, share, size, width), bf16) for _, size in chunks]
    factor = pltpu.VMEM((nblk, width, width), bf16)
    return pl.pallas_call(
        functools.partial(kernel, n_hi, n_lo, chunks),
        out_shape=jax.ShapeDtypeStruct((share, rows, width), bf16),
        in_specs=[pl.BlockSpec(memory_space=pltpu.SMEM)] + [pl.BlockSpec(memory_space=pl.ANY)] * 3,
        out_specs=pl.BlockSpec(memory_space=pltpu.VMEM),
        scratch_shapes=[whole] + pieces * 7 + shares + [factor] * 8 + [
            pltpu.SemaphoreType.DMA,
            pltpu.SemaphoreType.DMA((2, 4)),
            pltpu.SemaphoreType.DMA((3, count)),
            pltpu.SemaphoreType.DMA((3, count)),
            pltpu.SemaphoreType.DMA((n_hi - 1, count)),
            pltpu.SemaphoreType.DMA((n_hi - 1, count)),
        ],
        compiler_params=pltpu.CompilerParams(
            collective_id=0, has_side_effects=True, vmem_limit_bytes=56 * 1024 * 1024
        ),
        cost_estimate=pl.CostEstimate(
            flops=16 * nblk * rows * width * width,
            bytes_accessed=2 * (blocks.size + 8 * nblk * width * width + share * rows * width),
            transcendentals=0,
        ),
    )(partner_maps, blocks, diag_factors, off_factors)


def solution(mesh):
    in_specs = (
        P(("hi", "lo"), None, None),
        P(None, ("hi", "lo"), None, None),
        P(None, ("hi", "lo"), None, None),
        P(),
    )
    out_specs = P(("lo", "hi"), None, None)
    run = functools.partial(body, mesh.shape["hi"], mesh.shape["lo"])
    return jax.shard_map(run, mesh=mesh, in_specs=in_specs, out_specs=out_specs, check_vma=False)
```

```python
import functools

import jax
import jax.numpy as jnp
from jax import lax
from jax.experimental import pallas as pl
from jax.experimental.pallas import tpu as pltpu
from jax.sharding import PartitionSpec as P

MESH = pl.DeviceIdType.MESH
UNROLL = 16


def chunk_plan(rows):
    size = 16
    return tuple((start, size) for start in range(0, rows, size))


def order_of(count):
    steps = []
    begun = 0
    for c in range(count):
        while begun < min(count, c + 2 + (c >= 2)):
            steps.append((0, begun))
            begun += 1
        steps.append((1, c))
        if c >= 2:
            steps.append((2, c - 2))
    return steps + [(2, c) for c in range(max(count - 2, 0), count)]


def flip(index, step):
    return index + step * (1 - 2 * (lax.rem(lax.div(index, step), 2)))


def kernel(n_hi, n_lo, chunks, maps, blocks, diag, off, out, *scratch):
    count = len(chunks)
    scratch = list(scratch)

    def take(number):
        taken = scratch[:number]
        del scratch[:number]
        return taken

    x0, = take(1)
    xs = [None] + [take(count) for _ in range(3)]
    recv = [take(count) for _ in range(3)]
    partial = take(count)
    others = take(count)
    dfs = take(4)
    ofs = take(4)
    load_sem, factor_sem, send_sem, recv_sem, sum_send, sum_recv = scratch

    hi = lax.axis_index("hi")
    lo = lax.axis_index("lo")
    steps = (1, 2, n_lo // 2)
    nblk = blocks.shape[0]
    share = nblk // n_hi

    near = sorted(set(steps))
    lo_partner = {s: flip(lo, s) for s in near}
    hi_partner = [lax.rem(hi + d, n_hi) for d in range(1, n_hi)]
    barrier = pltpu.get_barrier_semaphore()
    for s in near:
        pl.semaphore_signal(barrier, inc=1, device_id=(hi, lo_partner[s]), device_id_type=MESH)
    for h in hi_partner:
        pl.semaphore_signal(barrier, inc=1, device_id=(h, lo), device_id_type=MESH)

    load_x = pltpu.make_async_copy(blocks, x0, load_sem)
    load_x.start()
    loads = []
    for k in range(4):
        loads.append((
            pltpu.make_async_copy(diag.at[k], dfs[k], factor_sem.at[0, k]),
            pltpu.make_async_copy(off.at[k], ofs[k], factor_sem.at[1, k]),
        ))
    for copy in loads[0]:
        copy.start()
    pl.semaphore_wait(barrier, len(near) + n_hi - 1)

    def exchange(level, c):
        start, size = chunks[c]
        source = blocks.at[:, pl.ds(start, size), :] if level == 0 else xs[level][c]
        return pltpu.make_async_remote_copy(
            src_ref=source,
            dst_ref=recv[level][c],
            send_sem=send_sem.at[level, c],
            recv_sem=recv_sem.at[level, c],
            device_id=(hi, lo_partner[steps[level]]),
            device_id_type=MESH,
        )

    def hand_on(c, d):
        return pltpu.make_async_remote_copy(
            src_ref=partial[c].at[pl.ds(hi_partner[d] * share, share)],
            dst_ref=others[c].at[d],
            send_sem=sum_send.at[d, c],
            recv_sem=sum_recv.at[d, c],
            device_id=(hi_partner[d], lo),
            device_id_type=MESH,
        )

    def product(left, right, d, o):
        return lax.dot_general(
            jnp.concatenate([left, right], axis=1),
            jnp.concatenate([d, o], axis=1),
            (((1,), (1,)), ((), ())),
            preferred_element_type=jnp.float32,
        ).astype(jnp.bfloat16)

    def over_blocks(number, one):
        unroll = UNROLL if number % UNROLL == 0 else 1

        def some(i, _):
            for u in range(unroll):
                one(i * unroll + u)
            return 0

        lax.fori_loop(0, number // unroll, some, 0)

    def mix(level, c):
        start, size = chunks[c]

        def one(j):
            mine = x0[j, pl.ds(start, size), :] if level == 0 else xs[level][c][j]
            theirs = recv[level][c][maps[level, j]]
            xs[level + 1][c][j] = product(mine, theirs, dfs[level][j], ofs[level][j])

        over_blocks(nblk, one)

    def last(c):
        def one(j):
            p = maps[3, j]
            partial[c][j] = product(xs[3][c][j], xs[3][c][p], dfs[3][j], ofs[3][p])

        over_blocks(nblk, one)

    def gather_sum(c):
        start, size = chunks[c]
        for d in range(n_hi - 1):
            hand_on(c, d).wait_recv()

        def one(i):
            total = partial[c][hi * share + i].astype(jnp.float32)
            for d in range(n_hi - 1):
                total = total + others[c][d, i].astype(jnp.float32)
            out[i, pl.ds(start, size), :] = total.astype(jnp.bfloat16)

        over_blocks(share, one)

    exchange(0, 0).start()
    for k in range(1, 4):
        for copy in loads[k]:
            copy.start()
    load_x.wait()
    loaded = set()
    pending = []
    for level, c in order_of(count):
        exchange(level, c).wait_recv()
        if level == 0:
            for later in (1, 2) if c == 0 else (c + 2,):
                if later < count:
                    exchange(0, later).start()
        if level not in loaded:
            for copy in loads[level]:
                copy.wait()
            loaded.add(level)
        mix(level, c)
        if level < 2:
            exchange(level + 1, c).start()
            continue
        if 3 not in loaded:
            for copy in loads[3]:
                copy.wait()
            loaded.add(3)
        last(c)
        for d in range(n_hi - 1):
            hand_on(c, d).start()
        for earlier in pending:
            gather_sum(earlier)
        pending = [c]
    for earlier in pending:
        gather_sum(earlier)
    for c in range(count):
        for level in range(3):
            exchange(level, c).wait_send()
        for d in range(n_hi - 1):
            hand_on(c, d).wait_send()


def body(n_hi, n_lo, blocks, diag_factors, off_factors, partner_maps):
    nblk, rows, width = blocks.shape
    chunks = chunk_plan(rows)
    count = len(chunks)
    share = nblk // n_hi
    bf16 = jnp.bfloat16
    whole = pltpu.VMEM((nblk, rows, width), bf16)
    pieces = [pltpu.VMEM((nblk, size, width), bf16) for _, size in chunks]
    shares = [pltpu.VMEM((n_hi - 1, share, size, width), bf16) for _, size in chunks]
    factor = pltpu.VMEM((nblk, width, width), bf16)
    return pl.pallas_call(
        functools.partial(kernel, n_hi, n_lo, chunks),
        out_shape=jax.ShapeDtypeStruct((share, rows, width), bf16),
        in_specs=[pl.BlockSpec(memory_space=pltpu.SMEM)] + [pl.BlockSpec(memory_space=pl.ANY)] * 3,
        out_specs=pl.BlockSpec(memory_space=pltpu.VMEM),
        scratch_shapes=[whole] + pieces * 7 + shares + [factor] * 8 + [
            pltpu.SemaphoreType.DMA,
            pltpu.SemaphoreType.DMA((2, 4)),
            pltpu.SemaphoreType.DMA((3, count)),
            pltpu.SemaphoreType.DMA((3, count)),
            pltpu.SemaphoreType.DMA((n_hi - 1, count)),
            pltpu.SemaphoreType.DMA((n_hi - 1, count)),
        ],
        compiler_params=pltpu.CompilerParams(
            collective_id=0, has_side_effects=True, vmem_limit_bytes=56 * 1024 * 1024
        ),
        cost_estimate=pl.CostEstimate(
            flops=16 * nblk * rows * width * width,
            bytes_accessed=2 * (blocks.size + 8 * nblk * width * width + share * rows * width),
            transcendentals=0,
        ),
    )(partner_maps, blocks, diag_factors, off_factors)


def solution(mesh):
    in_specs = (
        P(("hi", "lo"), None, None),
        P(None, ("hi", "lo"), None, None),
        P(None, ("hi", "lo"), None, None),
        P(),
    )
    out_specs = P(("lo", "hi"), None, None)
    run = functools.partial(body, mesh.shape["hi"], mesh.shape["lo"])
    return jax.shard_map(run, mesh=mesh, in_specs=in_specs, out_specs=out_specs, check_vma=False)
```

```python
import functools

import jax
import jax.numpy as jnp
from jax import lax
from jax.experimental import pallas as pl
from jax.experimental.pallas import tpu as pltpu
from jax.sharding import PartitionSpec as P

MESH = pl.DeviceIdType.MESH
UNROLL = 8


def chunk_plan(rows):
    size = 16
    return tuple((start, size) for start in range(0, rows, size))


def order_of(count):
    if count != 8:
        return [(level, (c,)) for c in range(count) for level in range(3)]
    return [
        (0, (0,)), (0, (1,)), (1, (0,)), (0, (2,)), (1, (1,)), (0, (3,)), (1, (2,)),
        (0, (4, 5)), (1, (3,)), (2, (0, 1)), (1, (4,)), (0, (6, 7)), (2, (2, 3)),
        (1, (5,)), (1, (6,)), (1, (7,)), (2, (4, 5)), (2, (6,)), (2, (7,)),
    ]


def issue_after(count):
    if count != 8:
        return {c: (c + 1,) for c in range(count - 1)}
    return {0: (1,), 1: (2,), 2: (3, 4), 3: (5, 6), 5: (7,)}


def flip(index, step):
    return index + step * (1 - 2 * (lax.rem(lax.div(index, step), 2)))


def kernel(n_hi, n_lo, chunks, maps, blocks, diag, off, out, *scratch):
    count = len(chunks)
    scratch = list(scratch)

    def take(number):
        taken = scratch[:number]
        del scratch[:number]
        return taken

    x0, = take(1)
    xs = [None] + [take(count) for _ in range(3)]
    recv = [take(count) for _ in range(3)]
    partial = take(count)
    others = take(count)
    dfs = take(4)
    ofs = take(4)
    load_sem, factor_sem, send_sem, recv_sem, sum_send, sum_recv = scratch

    hi = lax.axis_index("hi")
    lo = lax.axis_index("lo")
    steps = (1, 2, n_lo // 2)
    nblk = blocks.shape[0]
    share = nblk // n_hi

    near = sorted(set(steps))
    lo_partner = {s: flip(lo, s) for s in near}
    hi_partner = []
    for d in range(1, n_hi):
        other = hi
        for bit in range(n_hi.bit_length() - 1):
            other = flip(other, 1 << bit) if d >> bit & 1 else other
        hi_partner.append(other)
    barrier = pltpu.get_barrier_semaphore()
    for s in near:
        pl.semaphore_signal(barrier, inc=1, device_id=(hi, lo_partner[s]), device_id_type=MESH)
    for h in hi_partner:
        pl.semaphore_signal(barrier, inc=1, device_id=(h, lo), device_id_type=MESH)

    load_x = pltpu.make_async_copy(blocks, x0, load_sem)
    load_x.start()
    loads = []
    for k in range(4):
        loads.append((
            pltpu.make_async_copy(diag.at[k], dfs[k], factor_sem.at[0, k]),
            pltpu.make_async_copy(off.at[k], ofs[k], factor_sem.at[1, k]),
        ))
    for copy in loads[0]:
        copy.start()
    pl.semaphore_wait(barrier, len(near) + n_hi - 1)

    half = nblk // 2

    def exchange(level, c, part):
        start, size = chunks[c]
        own = pl.ds(part * half, half)
        source = blocks.at[own, pl.ds(start, size), :] if level == 0 else xs[level][c].at[own]
        return pltpu.make_async_remote_copy(
            src_ref=source,
            dst_ref=recv[level][c].at[own],
            send_sem=send_sem.at[level, c, part],
            recv_sem=recv_sem.at[level, c, part],
            device_id=(hi, lo_partner[steps[level]]),
            device_id_type=MESH,
        )

    def hand_on(c, d):
        return pltpu.make_async_remote_copy(
            src_ref=partial[c].at[pl.ds(hi_partner[d] * share, share)],
            dst_ref=others[c].at[d],
            send_sem=sum_send.at[d, c],
            recv_sem=sum_recv.at[d, c],
            device_id=(hi_partner[d], lo),
            device_id_type=MESH,
        )

    def product(pairs, d, o):
        rows = [jnp.concatenate(pair, axis=1) for pair in pairs]
        return lax.dot_general(
            jnp.concatenate(rows, axis=0),
            jnp.concatenate([d, o], axis=1),
            (((1,), (1,)), ((), ())),
            preferred_element_type=jnp.float32,
        ).astype(jnp.bfloat16)

    def over_blocks(first, number, one):
        unroll = UNROLL if number % UNROLL == 0 else 1

        def some(i, _):
            for u in range(unroll):
                one(first + i * unroll + u)
            return 0

        lax.fori_loop(0, number // unroll, some, 0)

    def put(targets, j, cs, value):
        row = 0
        for c in cs:
            size = chunks[c][1]
            targets[c][j] = value[row:row + size]
            row += size

    def mix(level, cs):
        def one(j):
            pairs = []
            for c in cs:
                start, size = chunks[c]
                mine = x0[j, pl.ds(start, size), :] if level == 0 else xs[level][c][j]
                pairs.append((mine, recv[level][c][maps[level, j]]))
            put(xs[level + 1], j, cs, product(pairs, dfs[level][j], ofs[level][j]))

        if level == 2:
            over_blocks(0, nblk, one)
            return
        for part in range(2):
            over_blocks(part * half, half, one)
            for c in cs:
                exchange(level + 1, c, part).start()

    def last(cs):
        def one(j):
            p = maps[3, j]
            pairs = [(xs[3][c][j], xs[3][c][p]) for c in cs]
            put(partial, j, cs, product(pairs, dfs[3][j], ofs[3][p]))

        for d in range(n_hi - 2, -1, -1):
            over_blocks(hi_partner[d] * share, share, one)
            for c in cs:
                hand_on(c, d).start()
        over_blocks(hi * share, share, one)

    def gather_sum(c):
        start, size = chunks[c]
        for d in range(n_hi - 2, -1, -1):
            hand_on(c, d).wait_recv()

        def one(i):
            total = partial[c][hi * share + i].astype(jnp.float32)
            for d in range(n_hi - 1):
                total = total + others[c][d, i].astype(jnp.float32)
            out[i, pl.ds(start, size), :] = total.astype(jnp.bfloat16)

        over_blocks(0, share, one)

    for part in range(2):
        exchange(0, 0, part).start()
    for k in range(1, 4):
        for copy in loads[k]:
            copy.start()
    load_x.wait()
    issue = issue_after(count)
    loaded = set()

    def ready(level):
        if level not in loaded:
            for copy in loads[level]:
                copy.wait()
            loaded.add(level)

    pending = ()
    for level, cs in order_of(count):
        for c in cs:
            for part in range(2):
                exchange(level, c, part).wait_recv()
            if level == 0:
                for later in issue.get(c, ()):
                    for part in range(2):
                        exchange(0, later, part).start()
        ready(level)
        mix(level, cs)
        if level == 2:
            ready(3)
            last(cs)
            for earlier in pending:
                gather_sum(earlier)
            pending = cs
    for earlier in pending:
        gather_sum(earlier)
    for c in range(count):
        for level in range(3):
            for part in range(2):
                exchange(level, c, part).wait_send()
        for d in range(n_hi - 1):
            hand_on(c, d).wait_send()


def body(n_hi, n_lo, blocks, diag_factors, off_factors, partner_maps):
    nblk, rows, width = blocks.shape
    chunks = chunk_plan(rows)
    count = len(chunks)
    share = nblk // n_hi
    bf16 = jnp.bfloat16
    whole = pltpu.VMEM((nblk, rows, width), bf16)
    pieces = [pltpu.VMEM((nblk, size, width), bf16) for _, size in chunks]
    shares = [pltpu.VMEM((n_hi - 1, share, size, width), bf16) for _, size in chunks]
    factor = pltpu.VMEM((nblk, width, width), bf16)
    return pl.pallas_call(
        functools.partial(kernel, n_hi, n_lo, chunks),
        out_shape=jax.ShapeDtypeStruct((share, rows, width), bf16),
        in_specs=[pl.BlockSpec(memory_space=pltpu.SMEM)] + [pl.BlockSpec(memory_space=pl.ANY)] * 3,
        out_specs=pl.BlockSpec(memory_space=pltpu.VMEM),
        scratch_shapes=[whole] + pieces * 7 + shares + [factor] * 8 + [
            pltpu.SemaphoreType.DMA,
            pltpu.SemaphoreType.DMA((2, 4)),
            pltpu.SemaphoreType.DMA((3, count, 2)),
            pltpu.SemaphoreType.DMA((3, count, 2)),
            pltpu.SemaphoreType.DMA((n_hi - 1, count)),
            pltpu.SemaphoreType.DMA((n_hi - 1, count)),
        ],
        compiler_params=pltpu.CompilerParams(
            collective_id=0, has_side_effects=True, vmem_limit_bytes=56 * 1024 * 1024
        ),
        cost_estimate=pl.CostEstimate(
            flops=16 * nblk * rows * width * width,
            bytes_accessed=2 * (blocks.size + 8 * nblk * width * width + share * rows * width),
            transcendentals=0,
        ),
    )(partner_maps, blocks, diag_factors, off_factors)


def solution(mesh):
    in_specs = (
        P(("hi", "lo"), None, None),
        P(None, ("hi", "lo"), None, None),
        P(None, ("hi", "lo"), None, None),
        P(),
    )
    out_specs = P(("lo", "hi"), None, None)
    run = functools.partial(body, mesh.shape["hi"], mesh.shape["lo"])
    return jax.shard_map(run, mesh=mesh, in_specs=in_specs, out_specs=out_specs, check_vma=False)
```

```python
import functools

import jax
import jax.numpy as jnp
from jax import lax
from jax.experimental import pallas as pl
from jax.experimental.pallas import tpu as pltpu
from jax.sharding import PartitionSpec as P

MESH = pl.DeviceIdType.MESH
UNROLL = 8


def chunk_plan(rows):
    size = 16
    return tuple((start, size) for start in range(0, rows, size))


def order_of(count):
    if count != 8:
        return [(level, (c,)) for c in range(count) for level in range(3)]
    return [
        (0, (0,)), (0, (1,)), (1, (0,)), (0, (2,)), (1, (1,)), (0, (3,)), (0, (4,)),
        (1, (2,)), (0, (5,)), (0, (6,)), (1, (3,)), (0, (7,)), (1, (4,)), (2, (0, 1)),
        (1, (5,)), (1, (6,)), (2, (2, 3)), (1, (7,)), (2, (4, 5)), (2, (6,)), (2, (7,)),
    ]


def issue_after(count):
    if count != 8:
        return {c: (c + 1,) for c in range(count - 1)}
    return {0: (1,), 1: (2, 3), 2: (4,), 3: (5,), 4: (6,), 5: (7,)}


def flip(index, step):
    return index + step * (1 - 2 * (lax.rem(lax.div(index, step), 2)))


def kernel(n_hi, n_lo, chunks, maps, blocks, diag, off, out, *scratch):
    count = len(chunks)
    scratch = list(scratch)

    def take(number):
        taken = scratch[:number]
        del scratch[:number]
        return taken

    x0, = take(1)
    xs = [None] + [take(count) for _ in range(3)]
    recv = [take(count) for _ in range(3)]
    partial = take(count)
    others = take(count)
    dfs = take(4)
    ofs = take(4)
    load_sem, factor_sem, send_sem, recv_sem, sum_send, sum_recv = scratch

    hi = lax.axis_index("hi")
    lo = lax.axis_index("lo")
    steps = (1, 2, n_lo // 2)
    nblk = blocks.shape[0]
    share = nblk // n_hi

    near = sorted(set(steps))
    lo_partner = {s: flip(lo, s) for s in near}
    hi_partner = []
    for d in range(1, n_hi):
        other = hi
        for bit in range(n_hi.bit_length() - 1):
            other = flip(other, 1 << bit) if d >> bit & 1 else other
        hi_partner.append(other)
    barrier = pltpu.get_barrier_semaphore()
    for s in near:
        pl.semaphore_signal(barrier, inc=1, device_id=(hi, lo_partner[s]), device_id_type=MESH)
    for h in hi_partner:
        pl.semaphore_signal(barrier, inc=1, device_id=(h, lo), device_id_type=MESH)

    load_x = pltpu.make_async_copy(blocks, x0, load_sem)
    load_x.start()
    loads = []
    for k in range(4):
        loads.append((
            pltpu.make_async_copy(diag.at[k], dfs[k], factor_sem.at[0, k]),
            pltpu.make_async_copy(off.at[k], ofs[k], factor_sem.at[1, k]),
        ))
    for copy in loads[0]:
        copy.start()
    pl.semaphore_wait(barrier, len(near) + n_hi - 1)

    half = nblk // 2

    def exchange(level, c, part):
        start, size = chunks[c]
        own = pl.ds(part * half, half)
        source = blocks.at[own, pl.ds(start, size), :] if level == 0 else xs[level][c].at[own]
        return pltpu.make_async_remote_copy(
            src_ref=source,
            dst_ref=recv[level][c].at[own],
            send_sem=send_sem.at[level, c, part],
            recv_sem=recv_sem.at[level, c, part],
            device_id=(hi, lo_partner[steps[level]]),
            device_id_type=MESH,
        )

    def hand_on(c, d):
        return pltpu.make_async_remote_copy(
            src_ref=partial[c].at[pl.ds(hi_partner[d] * share, share)],
            dst_ref=others[c].at[d],
            send_sem=sum_send.at[d, c],
            recv_sem=sum_recv.at[d, c],
            device_id=(hi_partner[d], lo),
            device_id_type=MESH,
        )

    def product(pairs, d, o):
        rows = [jnp.concatenate(pair, axis=1) for pair in pairs]
        return lax.dot_general(
            jnp.concatenate(rows, axis=0),
            jnp.concatenate([d, o], axis=1),
            (((1,), (1,)), ((), ())),
            preferred_element_type=jnp.float32,
        ).astype(jnp.bfloat16)

    def over_blocks(first, number, one):
        unroll = UNROLL if number % UNROLL == 0 else 1

        def some(i, _):
            for u in range(unroll):
                one(first + i * unroll + u)
            return 0

        lax.fori_loop(0, number // unroll, some, 0)

    def put(targets, j, cs, value):
        row = 0
        for c in cs:
            size = chunks[c][1]
            targets[c][j] = value[row:row + size]
            row += size

    def mix(level, cs):
        def one(j):
            pairs = []
            for c in cs:
                start, size = chunks[c]
                mine = x0[j, pl.ds(start, size), :] if level == 0 else xs[level][c][j]
                pairs.append((mine, recv[level][c][maps[level, j]]))
            put(xs[level + 1], j, cs, product(pairs, dfs[level][j], ofs[level][j]))

        if level == 2:
            over_blocks(0, nblk, one)
            return
        for part in range(2):
            over_blocks(part * half, half, one)
            for c in cs:
                exchange(level + 1, c, part).start()

    def last(cs):
        def one(j):
            p = maps[3, j]
            pairs = [(xs[3][c][j], xs[3][c][p]) for c in cs]
            put(partial, j, cs, product(pairs, dfs[3][j], ofs[3][p]))

        for d in range(n_hi - 2, -1, -1):
            over_blocks(hi_partner[d] * share, share, one)
            for c in cs:
                hand_on(c, d).start()
        over_blocks(hi * share, share, one)

    def gather_sum(c):
        start, size = chunks[c]
        for d in range(n_hi - 2, -1, -1):
            hand_on(c, d).wait_recv()

        def one(i):
            total = partial[c][hi * share + i].astype(jnp.float32)
            for d in range(n_hi - 1):
                total = total + others[c][d, i].astype(jnp.float32)
            out[i, pl.ds(start, size), :] = total.astype(jnp.bfloat16)

        over_blocks(0, share, one)

    for part in range(2):
        exchange(0, 0, part).start()
    for k in range(1, 4):
        for copy in loads[k]:
            copy.start()
    load_x.wait()
    issue = issue_after(count)
    loaded = set()

    def ready(level):
        if level not in loaded:
            for copy in loads[level]:
                copy.wait()
            loaded.add(level)

    pending = ()
    for level, cs in order_of(count):
        for c in cs:
            for part in range(2):
                exchange(level, c, part).wait_recv()
            if level == 0:
                for later in issue.get(c, ()):
                    for part in range(2):
                        exchange(0, later, part).start()
        ready(level)
        mix(level, cs)
        if level == 2:
            ready(3)
            last(cs)
            for earlier in pending:
                gather_sum(earlier)
            pending = cs
    for earlier in pending:
        gather_sum(earlier)
    for c in range(count):
        for level in range(3):
            for part in range(2):
                exchange(level, c, part).wait_send()
        for d in range(n_hi - 1):
            hand_on(c, d).wait_send()


def body(n_hi, n_lo, blocks, diag_factors, off_factors, partner_maps):
    nblk, rows, width = blocks.shape
    chunks = chunk_plan(rows)
    count = len(chunks)
    share = nblk // n_hi
    bf16 = jnp.bfloat16
    whole = pltpu.VMEM((nblk, rows, width), bf16)
    pieces = [pltpu.VMEM((nblk, size, width), bf16) for _, size in chunks]
    shares = [pltpu.VMEM((n_hi - 1, share, size, width), bf16) for _, size in chunks]
    factor = pltpu.VMEM((nblk, width, width), bf16)
    return pl.pallas_call(
        functools.partial(kernel, n_hi, n_lo, chunks),
        out_shape=jax.ShapeDtypeStruct((share, rows, width), bf16),
        in_specs=[pl.BlockSpec(memory_space=pltpu.SMEM)] + [pl.BlockSpec(memory_space=pl.ANY)] * 3,
        out_specs=pl.BlockSpec(memory_space=pltpu.VMEM),
        scratch_shapes=[whole] + pieces * 7 + shares + [factor] * 8 + [
            pltpu.SemaphoreType.DMA,
            pltpu.SemaphoreType.DMA((2, 4)),
            pltpu.SemaphoreType.DMA((3, count, 2)),
            pltpu.SemaphoreType.DMA((3, count, 2)),
            pltpu.SemaphoreType.DMA((n_hi - 1, count)),
            pltpu.SemaphoreType.DMA((n_hi - 1, count)),
        ],
        compiler_params=pltpu.CompilerParams(
            collective_id=0, has_side_effects=True, vmem_limit_bytes=56 * 1024 * 1024
        ),
        cost_estimate=pl.CostEstimate(
            flops=16 * nblk * rows * width * width,
            bytes_accessed=2 * (blocks.size + 8 * nblk * width * width + share * rows * width),
            transcendentals=0,
        ),
    )(partner_maps, blocks, diag_factors, off_factors)


def solution(mesh):
    in_specs = (
        P(("hi", "lo"), None, None),
        P(None, ("hi", "lo"), None, None),
        P(None, ("hi", "lo"), None, None),
        P(),
    )
    out_specs = P(("lo", "hi"), None, None)
    run = functools.partial(body, mesh.shape["hi"], mesh.shape["lo"])
    return jax.shard_map(run, mesh=mesh, in_specs=in_specs, out_specs=out_specs, check_vma=False)
```

```python
import functools

import jax
import jax.numpy as jnp
from jax import lax
from jax.experimental import pallas as pl
from jax.experimental.pallas import tpu as pltpu
from jax.sharding import PartitionSpec as P

MESH = pl.DeviceIdType.MESH
UNROLL = 16


def chunk_plan(rows):
    size = 16
    return tuple((start, size) for start in range(0, rows, size))


def order_of(count):
    if count != 8:
        return [(level, (c,)) for c in range(count) for level in range(3)]
    return [
        (0, (0,)), (0, (1,)), (1, (0,)), (0, (2,)), (1, (1,)), (0, (3,)), (0, (4,)),
        (1, (2,)), (0, (5,)), (0, (6,)), (1, (3,)), (0, (7,)), (1, (4,)), (2, (0, 1)),
        (1, (5,)), (1, (6,)), (2, (2, 3)), (1, (7,)), (2, (4, 5)), (2, (6,)), (2, (7,)),
    ]


def issue_after(count):
    if count != 8:
        return {c: (c + 1,) for c in range(count - 1)}
    return {0: (1,), 1: (2, 3), 2: (4,), 3: (5,), 4: (6,), 5: (7,)}


def flip(index, step):
    return index + step * (1 - 2 * (lax.rem(lax.div(index, step), 2)))


def kernel(n_hi, n_lo, chunks, maps, blocks, diag, off, out, *scratch):
    count = len(chunks)
    scratch = list(scratch)

    def take(number):
        taken = scratch[:number]
        del scratch[:number]
        return taken

    x0, = take(1)
    xs = [None] + [take(count) for _ in range(3)]
    recv = [take(count) for _ in range(3)]
    partial = take(count)
    others = take(count)
    dfs = take(4)
    ofs = take(4)
    load_sem, factor_sem, send_sem, recv_sem, sum_send, sum_recv = scratch

    hi = lax.axis_index("hi")
    lo = lax.axis_index("lo")
    steps = (1, 2, n_lo // 2)
    nblk = blocks.shape[0]
    share = nblk // n_hi

    near = sorted(set(steps))
    lo_partner = {s: flip(lo, s) for s in near}
    hi_partner = []
    for d in range(1, n_hi):
        other = hi
        for bit in range(n_hi.bit_length() - 1):
            other = flip(other, 1 << bit) if d >> bit & 1 else other
        hi_partner.append(other)
    barrier = pltpu.get_barrier_semaphore()
    for s in near:
        pl.semaphore_signal(barrier, inc=1, device_id=(hi, lo_partner[s]), device_id_type=MESH)
    for h in hi_partner:
        pl.semaphore_signal(barrier, inc=1, device_id=(h, lo), device_id_type=MESH)

    load_x = pltpu.make_async_copy(blocks, x0, load_sem)
    load_x.start()
    loads = []
    for k in range(4):
        loads.append((
            pltpu.make_async_copy(diag.at[k], dfs[k], factor_sem.at[0, k]),
            pltpu.make_async_copy(off.at[k], ofs[k], factor_sem.at[1, k]),
        ))
    for copy in loads[0]:
        copy.start()
    pl.semaphore_wait(barrier, len(near) + n_hi - 1)

    half = nblk // 2

    def exchange(level, c, part):
        start, size = chunks[c]
        own = pl.ds(part * half, half)
        source = blocks.at[own, pl.ds(start, size), :] if level == 0 else xs[level][c].at[own]
        return pltpu.make_async_remote_copy(
            src_ref=source,
            dst_ref=recv[level][c].at[own],
            send_sem=send_sem.at[level, c, part],
            recv_sem=recv_sem.at[level, c, part],
            device_id=(hi, lo_partner[steps[level]]),
            device_id_type=MESH,
        )

    def hand_on(c, d):
        return pltpu.make_async_remote_copy(
            src_ref=partial[c].at[pl.ds(hi_partner[d] * share, share)],
            dst_ref=others[c].at[d],
            send_sem=sum_send.at[d, c],
            recv_sem=sum_recv.at[d, c],
            device_id=(hi_partner[d], lo),
            device_id_type=MESH,
        )

    def product(pairs, d, o):
        rows = [jnp.concatenate(pair, axis=1) for pair in pairs]
        return lax.dot_general(
            jnp.concatenate(rows, axis=0),
            jnp.concatenate([d, o], axis=1),
            (((1,), (1,)), ((), ())),
            preferred_element_type=jnp.float32,
        ).astype(jnp.bfloat16)

    def over_blocks(first, number, one, store):
        unroll = UNROLL if number % UNROLL == 0 else 1

        def some(i, _):
            group = [first + i * unroll + u for u in range(unroll)]
            values = [one(j) for j in group]
            for j, value in zip(group, values):
                store(j, value)
            return 0

        lax.fori_loop(0, number // unroll, some, 0)

    def put(targets, j, cs, value):
        row = 0
        for c in cs:
            size = chunks[c][1]
            targets[c][j] = value[row:row + size]
            row += size

    def mix(level, cs):
        def one(j):
            pairs = []
            for c in cs:
                start, size = chunks[c]
                mine = x0[j, pl.ds(start, size), :] if level == 0 else xs[level][c][j]
                pairs.append((mine, recv[level][c][maps[level, j]]))
            return product(pairs, dfs[level][j], ofs[level][j])

        def store(j, value):
            put(xs[level + 1], j, cs, value)

        if level == 2:
            over_blocks(0, nblk, one, store)
            return
        for part in range(2):
            over_blocks(part * half, half, one, store)
            for c in cs:
                exchange(level + 1, c, part).start()

    def last(cs):
        def one(j):
            p = maps[3, j]
            pairs = [(xs[3][c][j], xs[3][c][p]) for c in cs]
            return product(pairs, dfs[3][j], ofs[3][p])

        def store(j, value):
            put(partial, j, cs, value)

        for d in range(n_hi - 2, -1, -1):
            over_blocks(hi_partner[d] * share, share, one, store)
            for c in cs:
                hand_on(c, d).start()
        over_blocks(hi * share, share, one, store)

    def gather_sum(c):
        start, size = chunks[c]
        for d in range(n_hi - 2, -1, -1):
            hand_on(c, d).wait_recv()

        def one(i):
            total = partial[c][hi * share + i].astype(jnp.float32)
            for d in range(n_hi - 1):
                total = total + others[c][d, i].astype(jnp.float32)
            return total.astype(jnp.bfloat16)

        def store(i, value):
            out[i, pl.ds(start, size), :] = value

        over_blocks(0, share, one, store)

    for part in range(2):
        exchange(0, 0, part).start()
    for k in range(1, 4):
        for copy in loads[k]:
            copy.start()
    load_x.wait()
    issue = issue_after(count)
    loaded = set()

    def ready(level):
        if level not in loaded:
            for copy in loads[level]:
                copy.wait()
            loaded.add(level)

    pending = ()
    for level, cs in order_of(count):
        for c in cs:
            for part in range(2):
                exchange(level, c, part).wait_recv()
            if level == 0:
                for later in issue.get(c, ()):
                    for part in range(2):
                        exchange(0, later, part).start()
        ready(level)
        mix(level, cs)
        if level == 2:
            ready(3)
            last(cs)
            for earlier in pending:
                gather_sum(earlier)
            pending = cs
    for earlier in pending:
        gather_sum(earlier)
    for c in range(count):
        for level in range(3):
            for part in range(2):
                exchange(level, c, part).wait_send()
        for d in range(n_hi - 1):
            hand_on(c, d).wait_send()


def body(n_hi, n_lo, blocks, diag_factors, off_factors, partner_maps):
    nblk, rows, width = blocks.shape
    chunks = chunk_plan(rows)
    count = len(chunks)
    share = nblk // n_hi
    bf16 = jnp.bfloat16
    whole = pltpu.VMEM((nblk, rows, width), bf16)
    pieces = [pltpu.VMEM((nblk, size, width), bf16) for _, size in chunks]
    shares = [pltpu.VMEM((n_hi - 1, share, size, width), bf16) for _, size in chunks]
    factor = pltpu.VMEM((nblk, width, width), bf16)
    return pl.pallas_call(
        functools.partial(kernel, n_hi, n_lo, chunks),
        out_shape=jax.ShapeDtypeStruct((share, rows, width), bf16),
        in_specs=[pl.BlockSpec(memory_space=pltpu.SMEM)] + [pl.BlockSpec(memory_space=pl.ANY)] * 3,
        out_specs=pl.BlockSpec(memory_space=pltpu.VMEM),
        scratch_shapes=[whole] + pieces * 7 + shares + [factor] * 8 + [
            pltpu.SemaphoreType.DMA,
            pltpu.SemaphoreType.DMA((2, 4)),
            pltpu.SemaphoreType.DMA((3, count, 2)),
            pltpu.SemaphoreType.DMA((3, count, 2)),
            pltpu.SemaphoreType.DMA((n_hi - 1, count)),
            pltpu.SemaphoreType.DMA((n_hi - 1, count)),
        ],
        compiler_params=pltpu.CompilerParams(
            collective_id=0, has_side_effects=True, vmem_limit_bytes=56 * 1024 * 1024
        ),
        cost_estimate=pl.CostEstimate(
            flops=16 * nblk * rows * width * width,
            bytes_accessed=2 * (blocks.size + 8 * nblk * width * width + share * rows * width),
            transcendentals=0,
        ),
    )(partner_maps, blocks, diag_factors, off_factors)


def solution(mesh):
    in_specs = (
        P(("hi", "lo"), None, None),
        P(None, ("hi", "lo"), None, None),
        P(None, ("hi", "lo"), None, None),
        P(),
    )
    out_specs = P(("lo", "hi"), None, None)
    run = functools.partial(body, mesh.shape["hi"], mesh.shape["lo"])
    return jax.shard_map(run, mesh=mesh, in_specs=in_specs, out_specs=out_specs, check_vma=False)
```

```python
import functools

import jax
import jax.numpy as jnp
from jax import lax
from jax.experimental import pallas as pl
from jax.experimental.pallas import tpu as pltpu
from jax.sharding import PartitionSpec as P

MESH = pl.DeviceIdType.MESH
UNROLL = 16


def chunk_plan(rows):
    size = 16
    return tuple((start, size) for start in range(0, rows, size))


def order_of(count):
    if count != 8:
        return [(level, (c,)) for c in range(count) for level in range(3)]
    return [
        (0, (0,)), (0, (1,)), (1, (0,)), (0, (2,)), (1, (1,)), (0, (3,)), (0, (4,)),
        (1, (2,)), (0, (5,)), (0, (6,)), (1, (3,)), (0, (7,)), (1, (4,)), (2, (0, 1)),
        (1, (5,)), (1, (6,)), (2, (2, 3)), (1, (7,)), (2, (4, 5)), (2, (6,)), (2, (7,)),
    ]


def issue_after(count):
    if count != 8:
        return {c: (c + 1,) for c in range(count - 1)}
    return {0: (1,), 1: (2, 3), 2: (4,), 3: (5,), 4: (6,), 5: (7,)}


def flip(index, step):
    return index + step * (1 - 2 * (lax.rem(lax.div(index, step), 2)))


def kernel(n_hi, n_lo, chunks, maps, blocks, diag, off, out, *scratch):
    count = len(chunks)
    scratch = list(scratch)

    def take(number):
        taken = scratch[:number]
        del scratch[:number]
        return taken

    x0, = take(1)
    xs = [None] + [take(count) for _ in range(3)]
    recv = [take(count) for _ in range(3)]
    partial = take(count)
    others = take(count)
    dfs = take(4)
    ofs = take(4)
    load_sem, factor_sem, send_sem, recv_sem, sum_send, sum_recv = scratch

    hi = lax.axis_index("hi")
    lo = lax.axis_index("lo")
    steps = (1, 2, n_lo // 2)
    nblk = blocks.shape[0]
    share = nblk // n_hi

    near = sorted(set(steps))
    lo_partner = {s: flip(lo, s) for s in near}
    hi_partner = []
    for d in range(1, n_hi):
        other = hi
        for bit in range(n_hi.bit_length() - 1):
            other = flip(other, 1 << bit) if d >> bit & 1 else other
        hi_partner.append(other)
    barrier = pltpu.get_barrier_semaphore()
    for s in near:
        pl.semaphore_signal(barrier, inc=1, device_id=(hi, lo_partner[s]), device_id_type=MESH)
    for h in hi_partner:
        pl.semaphore_signal(barrier, inc=1, device_id=(h, lo), device_id_type=MESH)

    load_x = pltpu.make_async_copy(blocks, x0, load_sem)
    load_x.start()
    loads = []
    for k in range(4):
        loads.append((
            pltpu.make_async_copy(diag.at[k], dfs[k], factor_sem.at[0, k]),
            pltpu.make_async_copy(off.at[k], ofs[k], factor_sem.at[1, k]),
        ))
    for copy in loads[0]:
        copy.start()
    pl.semaphore_wait(barrier, len(near) + n_hi - 1)

    half = nblk // 2

    def exchange(level, c, part):
        start, size = chunks[c]
        own = pl.ds(part * half, half)
        source = blocks.at[own, pl.ds(start, size), :] if level == 0 else xs[level][c].at[own]
        return pltpu.make_async_remote_copy(
            src_ref=source,
            dst_ref=recv[level][c].at[own],
            send_sem=send_sem.at[level, c, part],
            recv_sem=recv_sem.at[level, c, part],
            device_id=(hi, lo_partner[steps[level]]),
            device_id_type=MESH,
        )

    def hand_on(c, d):
        return pltpu.make_async_remote_copy(
            src_ref=partial[c].at[pl.ds(hi_partner[d] * share, share)],
            dst_ref=others[c].at[d],
            send_sem=sum_send.at[d, c],
            recv_sem=sum_recv.at[d, c],
            device_id=(hi_partner[d], lo),
            device_id_type=MESH,
        )

    def product(pairs, d, o):
        rows = [jnp.concatenate(pair, axis=1) for pair in pairs]
        return lax.dot_general(
            jnp.concatenate(rows, axis=0),
            jnp.concatenate([d, o], axis=0),
            (((1,), (0,)), ((), ())),
            preferred_element_type=jnp.float32,
        ).astype(jnp.bfloat16)

    def over_blocks(first, number, one, store):
        unroll = UNROLL if number % UNROLL == 0 else 1

        def some(i, _):
            group = [first + i * unroll + u for u in range(unroll)]
            values = [one(j) for j in group]
            for j, value in zip(group, values):
                store(j, value)
            return 0

        lax.fori_loop(0, number // unroll, some, 0)

    def turn(level):
        unroll = 4 if nblk % 4 == 0 else 1

        def some(i, _):
            for u in range(unroll):
                j = i * unroll + u
                dfs[level][j] = dfs[level][j].T
                ofs[level][j] = ofs[level][j].T
            return 0

        lax.fori_loop(0, nblk // unroll, some, 0)

    def put(targets, j, cs, value):
        row = 0
        for c in cs:
            size = chunks[c][1]
            targets[c][j] = value[row:row + size]
            row += size

    def mix(level, cs):
        def one(j):
            pairs = []
            for c in cs:
                start, size = chunks[c]
                mine = x0[j, pl.ds(start, size), :] if level == 0 else xs[level][c][j]
                pairs.append((mine, recv[level][c][maps[level, j]]))
            return product(pairs, dfs[level][j], ofs[level][j])

        def store(j, value):
            put(xs[level + 1], j, cs, value)

        if level == 2:
            over_blocks(0, nblk, one, store)
            return
        for part in range(2):
            over_blocks(part * half, half, one, store)
            for c in cs:
                exchange(level + 1, c, part).start()

    def last(cs):
        def one(j):
            p = maps[3, j]
            pairs = [(xs[3][c][j], xs[3][c][p]) for c in cs]
            return product(pairs, dfs[3][j], ofs[3][p])

        def store(j, value):
            put(partial, j, cs, value)

        for d in range(n_hi - 2, -1, -1):
            over_blocks(hi_partner[d] * share, share, one, store)
            for c in cs:
                hand_on(c, d).start()
        over_blocks(hi * share, share, one, store)

    def gather_sum(c):
        start, size = chunks[c]
        for d in range(n_hi - 2, -1, -1):
            hand_on(c, d).wait_recv()

        def one(i):
            total = partial[c][hi * share + i].astype(jnp.float32)
            for d in range(n_hi - 1):
                total = total + others[c][d, i].astype(jnp.float32)
            return total.astype(jnp.bfloat16)

        def store(i, value):
            out[i, pl.ds(start, size), :] = value

        over_blocks(0, share, one, store)

    for part in range(2):
        exchange(0, 0, part).start()
    for k in range(1, 4):
        for copy in loads[k]:
            copy.start()
    load_x.wait()
    issue = issue_after(count)
    loaded = set()

    def ready(level):
        if level not in loaded:
            for copy in loads[level]:
                copy.wait()
            loaded.add(level)
            turn(level)

    ready(0)
    pending = ()
    for level, cs in order_of(count):
        for c in cs:
            for part in range(2):
                exchange(level, c, part).wait_recv()
            if level == 0:
                for later in issue.get(c, ()):
                    for part in range(2):
                        exchange(0, later, part).start()
        ready(level)
        mix(level, cs)
        early = {(0, 0): 1, (1, 1): 2, (1, 3): 3}.get((level, cs[0]))
        if early is not None:
            ready(early)
        if level == 2:
            ready(3)
            last(cs)
            for earlier in pending:
                gather_sum(earlier)
            pending = cs
    for earlier in pending:
        gather_sum(earlier)
    for c in range(count):
        for level in range(3):
            for part in range(2):
                exchange(level, c, part).wait_send()
        for d in range(n_hi - 1):
            hand_on(c, d).wait_send()


def body(n_hi, n_lo, blocks, diag_factors, off_factors, partner_maps):
    nblk, rows, width = blocks.shape
    chunks = chunk_plan(rows)
    count = len(chunks)
    share = nblk // n_hi
    bf16 = jnp.bfloat16
    whole = pltpu.VMEM((nblk, rows, width), bf16)
    pieces = [pltpu.VMEM((nblk, size, width), bf16) for _, size in chunks]
    shares = [pltpu.VMEM((n_hi - 1, share, size, width), bf16) for _, size in chunks]
    factor = pltpu.VMEM((nblk, width, width), bf16)
    return pl.pallas_call(
        functools.partial(kernel, n_hi, n_lo, chunks),
        out_shape=jax.ShapeDtypeStruct((share, rows, width), bf16),
        in_specs=[pl.BlockSpec(memory_space=pltpu.SMEM)] + [pl.BlockSpec(memory_space=pl.ANY)] * 3,
        out_specs=pl.BlockSpec(memory_space=pltpu.VMEM),
        scratch_shapes=[whole] + pieces * 7 + shares + [factor] * 8 + [
            pltpu.SemaphoreType.DMA,
            pltpu.SemaphoreType.DMA((2, 4)),
            pltpu.SemaphoreType.DMA((3, count, 2)),
            pltpu.SemaphoreType.DMA((3, count, 2)),
            pltpu.SemaphoreType.DMA((n_hi - 1, count)),
            pltpu.SemaphoreType.DMA((n_hi - 1, count)),
        ],
        compiler_params=pltpu.CompilerParams(
            collective_id=0, has_side_effects=True, vmem_limit_bytes=56 * 1024 * 1024
        ),
        cost_estimate=pl.CostEstimate(
            flops=16 * nblk * rows * width * width,
            bytes_accessed=2 * (blocks.size + 8 * nblk * width * width + share * rows * width),
            transcendentals=0,
        ),
    )(partner_maps, blocks, diag_factors, off_factors)


def solution(mesh):
    in_specs = (
        P(("hi", "lo"), None, None),
        P(None, ("hi", "lo"), None, None),
        P(None, ("hi", "lo"), None, None),
        P(),
    )
    out_specs = P(("lo", "hi"), None, None)
    run = functools.partial(body, mesh.shape["hi"], mesh.shape["lo"])
    return jax.shard_map(run, mesh=mesh, in_specs=in_specs, out_specs=out_specs, check_vma=False)
```
